32 devices in a mesh: space: 8 (over z, y), snap: 4 (over x, core).
Axes of the slice: x: 2, y: 2, z: 4, core: 2. Of those that a mesh axis runs over, the one named last changes fastest.
Arguments:
- primal: bfloat16 [2048, 98304], P('snap', 'space'), may hold values from -6 to 6
- adjoint_pencils: bfloat16 [1024, 98304], P('snap', 'space'), may hold values from -0.02734375 to 0.02734375
- weights: float32 [98304], P('space'), may hold values from 0.2 to 2
- pencil_map: int32 [768], replicated, may hold values from 0 to 767, as said below
Outputs:
- hankel: float32 [1024, 2048], P('space', 'snap')
The draws below stay inside these ranges and needn't reach their ends.
Inputs may be any that keep to these rules, and one draw needn't show every extreme that they name: `pencil_map`: each number appears once; each aligned block of 96 entries holds exactly 12 entries from every aligned range of 96 values.
All inputs are finite; a program needn't handle non-finite values.
Results may differ from the reference program's by a relative error of at most 0.0029.
Values may be sent and summed in bfloat16 or wider, within the bound.
No kernel may reach another device: no remote copies, remote signals or barrier semaphores. Data moves between devices by JAX's collectives and lax.ppermute only.
A program may use at most 128 MiB of HBM per device.

```python
import math
import jax
import jax.numpy as jnp
from jax import lax

MP = 2048
MA = 1024
PEN_LEN = 128
PEN_DEV = 96
PENCILS = 768
NPTS = 98304


def draw_pencil_map(key, part):
    tiles = PENCILS // PEN_DEV
    share = PEN_DEV // tiles

    def shuffle(subkey):
        return jax.random.permutation(subkey, PEN_DEV)
    inner = jax.vmap(shuffle)(jax.random.split(jax.random.fold_in(key, 11), tiles)).astype(jnp.int32)
    slots = inner + (jnp.arange(tiles, dtype=jnp.int32) * PEN_DEV)[:, None]
    grouped = slots.reshape(tiles, tiles, share).transpose(1, 0, 2).reshape(tiles, PEN_DEV)
    mixing = jax.vmap(shuffle)(jax.random.split(jax.random.fold_in(key, 23), tiles)).astype(jnp.int32)
    return jnp.take_along_axis(grouped, mixing, axis=1).reshape(PENCILS).astype(jnp.int32)


def with_spikes(result, rng, source, target, blocks, factor):
    def block_of(position):
        return (jnp.arange(result.shape[position]) // (result.shape[position] // blocks)).reshape((-1,) + (1,) * (result.ndim - 1 - position))

    one_side = jax.random.permutation(rng, blocks)[block_of(target)]
    other_side = (block_of(target) + blocks // 2) % blocks
    return jnp.where((block_of(source) == one_side) | (block_of(source) == other_side), factor * result, result)


def levels(key, extent, pieces, smallest, largest):
    def one(axis_at, shards_of):
        heights = jax.random.uniform(jax.random.fold_in(jax.random.fold_in(key, 6), axis_at), (shards_of,), jnp.float32, smallest / len(pieces), largest / len(pieces))
        return jnp.repeat(jnp.exp(heights), extent[axis_at] // shards_of).reshape((-1,) + (1,) * (len(extent) - axis_at - 1))

    gain = one(*pieces[0])
    for cut in pieces[1:]:
        gain = gain * one(*cut)
    return gain


def centred(key, shape, scale, reach, cuts=(), held_as=jnp.bfloat16):
    level = levels(key, shape, cuts, -0.22, 0.18) if cuts else 1.0
    drawn = jax.random.normal(key, shape, jnp.float32) * scale * level
    return jnp.minimum(jnp.maximum(drawn, -reach), reach).astype(held_as)


def bell_draw_with(key, dims, spread, bound, pieces, heavy, kind=jnp.bfloat16):
    drawn = spread * jax.random.normal(key, dims, jnp.float32)
    if pieces:
        drawn = drawn * levels(key, dims, pieces, -0.22, 0.18)
    return jnp.clip(with_spikes(drawn, jax.random.fold_in(key, 3), *heavy), -bound, bound).astype(kind)


def setup_inputs(seed: int = 0) -> dict:
    arg_keys = jax.random.split(jax.random.key(seed), 5)
    primal = centred(arg_keys[0], (MP, NPTS), 1.0, 6.0, ((0, 4), (1, 8)))
    adjoint_pencils = bell_draw_with(arg_keys[1], (MA, NPTS), NPTS ** -0.5, 0.02734375, ((0, 4), (1, 8)), (1, 0, 8, 2.0))
    weights = jnp.clip(jnp.exp(math.log(2.0) - 2.3025851 * jax.random.uniform(arg_keys[2], (NPTS,), jnp.float32) ** levels(arg_keys[2], (NPTS,), ((0, 8),), -0.2, 0.2)), 0.2, 2.0)
    pencil_map = draw_pencil_map(jax.random.fold_in(arg_keys[4], 71), 0)
    return {"primal": primal, "adjoint_pencils": adjoint_pencils, "weights": weights, "pencil_map": pencil_map}


def reference(primal, adjoint_pencils, weights, pencil_map):
    weighted = (primal.astype(jnp.float32) * weights[None, :]).astype(jnp.bfloat16)
    blocks = adjoint_pencils.reshape(MA, PENCILS, PEN_LEN)
    tiled = jnp.zeros_like(blocks).at[:, pencil_map, :].set(blocks).reshape(MA, NPTS)
    return lax.dot_general(tiled, weighted, (((1,), (1,)), ((), ())), preferred_element_type=jnp.float32)
```

```python
import jax
import jax.numpy as jnp
from jax import lax
from jax.experimental import pallas as pl
from jax.experimental.pallas import tpu as pltpu
from jax.sharding import PartitionSpec as P

PEN_LEN = 128
ROWS = 16
COST_SCALE = 1


def xor_send(x, axis, k):
    n = lax.axis_size(axis)
    return lax.ppermute(x, axis, [(i, i ^ k) for i in range(n)])


def params(mebibytes=16):
    return pltpu.CompilerParams(vmem_limit_bytes=mebibytes * 1024 * 1024)


def cost(flops, nbytes):
    return pl.CostEstimate(flops=flops // COST_SCALE, bytes_accessed=nbytes // COST_SCALE, transcendentals=0)


def pack(adjoint, pencil_map, where, first, count, ks, tiles):
    halves, _, points = adjoint.shape
    pen_dev = points // PEN_LEN
    share = pen_dev // tiles

    def body(map_ref, where_ref, in_ref, *refs):
        outs, (table, seen) = refs[: len(ks)], refs[len(ks) :]
        place = where_ref[0]
        for k in range(tiles):
            seen[k] = 0

        def enter(q, carry):
            k = lax.div(map_ref[place * pen_dev + q], pen_dev) ^ place
            t = seen[k]
            seen[k] = t + 1
            table[k * share + t] = q
            return carry

        lax.fori_loop(0, pen_dev, enter, 0)
        for o, k in enumerate(ks):
            for t in range(share):
                start = pl.multiple_of(table[k * share + t] * PEN_LEN, PEN_LEN)
                for h in range(halves):
                    outs[o][h * count : (h + 1) * count, t * PEN_LEN : (t + 1) * PEN_LEN] = in_ref[
                        h, first : first + count, pl.ds(start, PEN_LEN)
                    ]

    smem, vmem = pl.BlockSpec(memory_space=pltpu.SMEM), pl.BlockSpec(memory_space=pltpu.VMEM)
    return pl.pallas_call(
        body,
        in_specs=[smem, smem, vmem],
        out_specs=[vmem] * len(ks),
        out_shape=[jax.ShapeDtypeStruct((halves * count, share * PEN_LEN), jnp.bfloat16)] * len(ks),
        scratch_shapes=[pltpu.SMEM((pen_dev,), jnp.int32), pltpu.SMEM((tiles,), jnp.int32)],
        compiler_params=params(),
        cost_estimate=cost(0, 4 * halves * count * points),
    )(pencil_map, where, adjoint)


def slots_of(pencil_map, place, tiles):
    pen_dev = pencil_map.shape[0] // tiles
    share = pen_dev // tiles
    local = pencil_map.reshape(tiles, pen_dev) - place * pen_dev
    here = (local >= 0) & (local < pen_dev)
    q = jnp.arange(pen_dev)
    rank = jnp.sum(here[:, None, :] & (q[None, None, :] < q[None, :, None]), axis=2)
    match = here[:, None, :] & (rank[:, None, :] == jnp.arange(share)[None, :, None])
    table = jnp.sum(jnp.where(match, local[:, None, :], 0), axis=2)
    order = jnp.arange(tiles) ^ place
    picked = jnp.sum(jnp.where(order[:, None, None] == jnp.arange(tiles)[None, :, None], table[None], 0), axis=1)
    return picked.reshape(pen_dev).astype(jnp.int32)


def weigh(primal, weights, table, first, count, tiles):
    rows, points = primal.shape
    share = points // PEN_LEN // tiles
    step = 64 if rows % 64 == 0 else rows

    def body(table_ref, in_ref, w_ref, out):
        for k in range(count):
            for t in range(share):
                start = pl.multiple_of(table_ref[(first + k) * share + t] * PEN_LEN, PEN_LEN)
                scale = w_ref[:, pl.ds(start, PEN_LEN)]
                for i in range(0, rows, step):
                    tile = in_ref[i : i + step, pl.ds(start, PEN_LEN)].astype(jnp.float32) * scale
                    out[k, i : i + step, t * PEN_LEN : (t + 1) * PEN_LEN] = tile.astype(jnp.bfloat16)

    vmem = pl.BlockSpec(memory_space=pltpu.VMEM)
    return pl.pallas_call(
        body,
        in_specs=[pl.BlockSpec(memory_space=pltpu.SMEM), vmem, vmem],
        out_specs=vmem,
        out_shape=jax.ShapeDtypeStruct((count, rows, share * PEN_LEN), jnp.bfloat16),
        compiler_params=params(),
        cost_estimate=cost(rows * points // 2, 3 * rows * points),
    )(table, primal, weights.reshape(1, points))


def merge(parts):
    n = len(parts)
    rows, depth = parts[0].shape
    step = rows // 2 if rows % (2 * ROWS) == 0 else rows

    def body(*refs):
        for i in range(n):
            refs[n][i] = refs[i][...]

    return pl.pallas_call(
        body,
        grid=(rows // step,),
        in_specs=[pl.BlockSpec((step, depth), lambda i: (i, 0))] * n,
        out_specs=pl.BlockSpec((n, step, depth), lambda i: (0, i, 0)),
        out_shape=jax.ShapeDtypeStruct((n, rows, depth), parts[0].dtype),
        compiler_params=params(),
        cost_estimate=cost(0, 4 * n * rows * depth),
    )(*parts)


def multiply(groups, own, other, where, before, each, halves, members):
    held = members // 2
    last = before is not None
    depth = groups[0][0][0].shape[-1]
    columns = own.shape[1]
    counts = [g[0][0].shape[0] if g[0][0].ndim == 3 else 1 for g in groups]
    flat = [a for g in groups for a in g[0]]
    rows = halves * each

    def body(where_ref, *refs):
        ins, w_refs = refs[: len(flat)], refs[len(flat) : len(flat) + 2]
        rest = refs[len(flat) + 2 :]
        total = rest[-1] if last else rest[0]
        if last:
            for n in range(held):
                for h in range(halves):
                    at = n * rows + h * each
                    from_row = h * before[0].shape[1] // halves + before[1]
                    total[at : at + each, :] = rest[0][n, from_row : from_row + each, :]
        k = 0
        for g, count in enumerate(counts):
            stride, first = groups[g][1:]
            for i in range(count):
                taken = []
                for ref in ins[g * held : (g + 1) * held]:
                    for h in range(halves):
                        span = slice(h * stride + first, h * stride + first + each)
                        taken.append(ref[i, span, :] if len(ref.shape) == 3 else ref[span, :])
                stacked = jnp.concatenate(taken, axis=0)
                for side in range(2):
                    product = lax.dot_general(
                        stacked, w_refs[side][k], (((1,), (1,)), ((), ())), preferred_element_type=jnp.float32
                    )
                    span = slice(side * columns, (side + 1) * columns)
                    if last:
                        total[:, span] += product
                    else:
                        for n in range(held):
                            value = product[n * rows : (n + 1) * rows]
                            total[n, :, span] = value if k == 0 else total[n, :, span] + value
                k += 1
        if last:
            for n in range(held):
                for h in range(halves):
                    e = ((where_ref[1] ^ (2 * n)) * halves + h) ^ where_ref[0]
                    to = lax.div(e, 2 * halves) * halves + lax.rem(e, halves)
                    at = (n * halves + h) * each
                    for side in range(2):
                        rest[1 + side][to] = total[at : at + each, side * columns : (side + 1) * columns]

    vmem = pl.BlockSpec(memory_space=pltpu.VMEM)
    full = jax.ShapeDtypeStruct((held, rows, 2 * columns), jnp.float32)
    split = [jax.ShapeDtypeStruct((held * halves, each, columns), jnp.float32)] * 2
    return pl.pallas_call(
        body,
        in_specs=[pl.BlockSpec(memory_space=pltpu.SMEM)] + [vmem] * (len(flat) + 2 + last),
        out_specs=[vmem, vmem] if last else vmem,
        out_shape=split if last else full,
        scratch_shapes=[pltpu.VMEM((held * rows, 2 * columns), jnp.float32)] if last else [],
        compiler_params=params(),
        cost_estimate=cost(
            4 * held * rows * columns * depth * sum(counts), 2 * sum(counts) * depth * (held * rows + 2 * columns)
        ),
    )(where, *flat, own, other, *((before[0],) if last else ()))


def after(x, *done):
    return lax.optimization_barrier((x,) + done)[0] if done else x


def on_device(primal, adjoint_pencils, weights, pencil_map):
    rows_here, points = adjoint_pencils.shape
    tiles = lax.axis_size("space")
    members = lax.axis_size("snap")
    place, lane = lax.axis_index("space"), lax.axis_index("snap")
    where = jnp.stack([place, lane]).astype(jnp.int32)
    rows_out = rows_here * members // tiles
    halves = rows_here // rows_out
    adjoint = adjoint_pencils.reshape(halves, rows_out, points)
    half = tiles // 2
    middle = half + half // 2
    units = rows_out // ROWS
    rows_a = units // 2 * ROWS
    rows_b = max(1, 3 * units // 8) * ROWS
    rows_c = rows_out - rows_a - rows_b
    table = slots_of(pencil_map, place, tiles)

    def pack_rows(source, first, count, ks):
        return dict(zip(ks, pack(source, pencil_map, where, first, count, ks, tiles)))

    def over_space(packed, ks, *done):
        return [xor_send(after(packed[k], *done), "space", k) for k in ks]

    def join(found):
        return found[0] if len(found) == 1 else merge(found)

    def across(block, *done):
        found, bit = [block], members // 2
        order = [0]
        while bit > 1:
            found = found + [xor_send(after(b, *done), "snap", bit) for b in found]
            order = order + [n ^ bit for n in order]
            bit //= 2
        return [found[order.index(n)] for n in sorted(order)]

    def spread(mine, got):
        same = (((lane * halves) ^ place) & halves) == 0
        shape = (-1, halves) + mine.shape[1:]
        mine, got = mine.reshape(shape), got.reshape(shape)
        both = jnp.stack([jnp.where(same, mine, got), jnp.where(same, got, mine)], axis=1)
        return both.reshape((-1,) + mine.shape[2:])

    def add_up(pair, *done):
        x = spread(pair[0], xor_send(after(pair[1], *done), "snap", 1))
        bit = 1
        steps = []
        while bit < tiles:
            x = x[0::2] + xor_send(x[1::2], "space", bit)
            steps.append(x)
            bit *= 2
        return steps

    near_a, near_b = list(range(2, 2 + (half - 2) // 2)), list(range(2 + (half - 2) // 2, half))
    low, high = list(range(half, middle)), list(range(middle, tiles))

    start_low, rest_low = low[: len(low) // 2], low[len(low) // 2 :]
    packed_a = pack_rows(adjoint, 0, rows_a, low)
    packed_n = pack_rows(after(adjoint, packed_a[low[0]]), 0, rows_out, list(range(half)))
    low_a = over_space(packed_a, start_low)
    near_1 = over_space(packed_n, [1])[0]
    got_na = over_space(packed_n, near_a)
    cross_0 = across(packed_n[0])
    own_near = weigh(after(primal, packed_n[0]), weights, table, 0, half, tiles)
    own_far = weigh(after(primal, own_near), weights, table, half, half, tiles)

    done = (*low_a, near_1, *got_na, cross_0[-1], own_far)
    low_a = low_a + over_space(packed_a, rest_low, *done)
    got_nb = over_space(packed_n, near_b, *done)
    cross_1 = across(near_1, *done)
    other_near = xor_send(after(own_near, *done), "snap", 1)
    other_far = xor_send(after(own_far, *done), "snap", 1)
    packed_ah = pack_rows(after(adjoint, own_far), 0, rows_a, high)
    packed_bc = pack_rows(after(adjoint, packed_ah[high[0]]), rows_a, rows_b + rows_c, low)
    packed_b = pack_rows(after(adjoint, packed_bc[low[0]]), rows_a, rows_b, high)
    packed_c = pack_rows(after(adjoint, packed_b[high[0]]), rows_a + rows_b, rows_c, high)

    done = (*low_a, *got_nb, cross_1[-1], other_near, other_far, packed_c[high[0]])
    high_a = over_space(packed_ah, high, *done)
    cross_low_a = across(join(low_a), *done)
    cross_na = across(join(got_na), *done)

    done = (*high_a, cross_low_a[-1], cross_na[-1])
    low_bc = over_space(packed_bc, low, *done)
    cross_nb = across(join(got_nb), *done)
    cross_high_a = across(join(high_a), *done)

    done = (*low_bc, cross_nb[-1], cross_high_a[-1])
    high_b = over_space(packed_b, high, *done)
    cross_low_bc = across(join(low_bc), *done)
    groups = [(g, rows_out, 0) for g in (cross_0, cross_1, cross_na, cross_nb)]
    product = multiply(groups, own_near, after(other_near, *done), where, None, rows_out, halves, members)
    groups = [(cross_low_a, rows_a, 0), (cross_high_a, rows_a, 0)]
    pair_a = multiply(groups, own_far, other_far, where, (product, 0), rows_a, halves, members)

    done = (*high_b, cross_low_bc[-1], pair_a[0])
    high_c = over_space(packed_c, high, *done)
    cross_high_b = across(join(high_b), *done)
    sums_a = add_up(pair_a, *done)

    done = (*high_c, cross_high_b[-1], sums_a[0])
    cross_high_c = across(join(high_c), *done)
    groups = [(cross_low_bc, rows_b + rows_c, 0), (cross_high_b, rows_b, 0)]
    pair_b = multiply(groups, own_far, other_far, where, (product, rows_a), rows_b, halves, members)
    sums_b = add_up(pair_b)
    groups = [(cross_low_bc, rows_b + rows_c, rows_b), (cross_high_c, rows_c, 0)]
    pair_c = multiply(groups, own_far, other_far, where, (product, rows_a + rows_b), rows_c, halves, members)
    sums_c = add_up(pair_c)
    return jnp.concatenate([sums_a[-1][0], sums_b[-1][0], sums_c[-1][0]], axis=0)


def solution(mesh):
    placed = (P("snap", "space"), P("snap", "space"), P("space"), P())
    return jax.shard_map(
        on_device, mesh=mesh, in_specs=placed, out_specs=P("space", "snap"), check_vma=False
    )
```

```python
import jax
import jax.numpy as jnp
from jax import lax
from jax.experimental import pallas as pl
from jax.experimental.pallas import tpu as pltpu
from jax.sharding import PartitionSpec as P

PEN_LEN = 128
ROWS = 16
COST_SCALE = 1
LIMIT = 50


def xor_send(x, axis, k):
    n = lax.axis_size(axis)
    return lax.ppermute(x, axis, [(i, i ^ k) for i in range(n)])


def params(mebibytes=8):
    return pltpu.CompilerParams(vmem_limit_bytes=mebibytes * 1024 * 1024)


def cost(flops, nbytes):
    return pl.CostEstimate(flops=flops // COST_SCALE, bytes_accessed=nbytes // COST_SCALE, transcendentals=0)


def pack(adjoint, table, where, first, count, ks, tiles):
    halves, _, points = adjoint.shape
    pen_dev = points // PEN_LEN
    share = pen_dev // tiles
    build = table.shape[0] != pen_dev
    magic = (1 << 20) // pen_dev + 1
    exact = all(x * magic >> 20 == x // pen_dev for x in range(tiles * pen_dev))

    def body(table_ref, where_ref, in_ref, *refs):
        outs = refs[: len(ks)]
        if build:
            made, seen = refs[len(ks) :]
            place = where_ref[0]
            for k in range(tiles):
                seen[k] = 0

            def enter(q, carry):
                slot = table_ref[place * pen_dev + q]
                k = (slot * magic >> 20 if exact else lax.div(slot, pen_dev)) ^ place
                t = seen[k]
                seen[k] = t + 1
                made[k * share + t] = q
                return carry

            lax.fori_loop(0, pen_dev, enter, 0, unroll=8)
        else:
            made = table_ref
        for o, k in enumerate(ks):
            for t in range(share):
                start = pl.multiple_of(made[k * share + t] * PEN_LEN, PEN_LEN)
                for h in range(halves):
                    outs[o][h * count : (h + 1) * count, t * PEN_LEN : (t + 1) * PEN_LEN] = in_ref[
                        h, first : first + count, pl.ds(start, PEN_LEN)
                    ]

    smem, vmem = pl.BlockSpec(memory_space=pltpu.SMEM), pl.BlockSpec(memory_space=pltpu.VMEM)
    return pl.pallas_call(
        body,
        in_specs=[smem, smem, vmem],
        out_specs=[vmem] * len(ks) + [smem] * build,
        out_shape=[jax.ShapeDtypeStruct((halves * count, share * PEN_LEN), jnp.bfloat16)] * len(ks)
        + [jax.ShapeDtypeStruct((pen_dev,), jnp.int32)] * build,
        scratch_shapes=[pltpu.SMEM((tiles,), jnp.int32)] * build,
        compiler_params=params(),
        cost_estimate=cost(0, 4 * halves * count * points),
    )(table, where, adjoint)


def slots_of(pencil_map, place, tiles):
    pen_dev = pencil_map.shape[0] // tiles
    share = pen_dev // tiles
    local = pencil_map.reshape(tiles, pen_dev) - place * pen_dev
    here = (local >= 0) & (local < pen_dev)
    q = jnp.arange(pen_dev)
    rank = jnp.sum(here[:, None, :] & (q[None, None, :] < q[None, :, None]), axis=2)
    match = here[:, None, :] & (rank[:, None, :] == jnp.arange(share)[None, :, None])
    table = jnp.sum(jnp.where(match, local[:, None, :], 0), axis=2)
    order = jnp.arange(tiles) ^ place
    picked = jnp.sum(jnp.where(order[:, None, None] == jnp.arange(tiles)[None, :, None], table[None], 0), axis=1)
    return picked.reshape(pen_dev).astype(jnp.int32)


def weigh(primal, weights, table, first, count, tiles):
    rows, points = primal.shape
    share = points // PEN_LEN // tiles
    step = 64 if rows % 64 == 0 else rows

    def body(table_ref, in_ref, w_ref, out):
        for k in range(count):
            for t in range(share):
                start = pl.multiple_of(table_ref[(first + k) * share + t] * PEN_LEN, PEN_LEN)
                scale = w_ref[:, pl.ds(start, PEN_LEN)]
                for i in range(0, rows, step):
                    tile = in_ref[i : i + step, pl.ds(start, PEN_LEN)].astype(jnp.float32) * scale
                    out[k, i : i + step, t * PEN_LEN : (t + 1) * PEN_LEN] = tile.astype(jnp.bfloat16)

    vmem = pl.BlockSpec(memory_space=pltpu.VMEM)
    return pl.pallas_call(
        body,
        in_specs=[pl.BlockSpec(memory_space=pltpu.SMEM), vmem, vmem],
        out_specs=vmem,
        out_shape=jax.ShapeDtypeStruct((count, rows, share * PEN_LEN), jnp.bfloat16),
        compiler_params=params(),
        cost_estimate=cost(rows * points // 2, 3 * rows * points),
    )(table, primal, weights.reshape(1, points))


def merge(parts):
    n = len(parts)
    rows, depth = parts[0].shape
    step = rows // 2 if rows % (2 * ROWS) == 0 else rows

    def body(*refs):
        for i in range(n):
            refs[n][i] = refs[i][...]

    return pl.pallas_call(
        body,
        grid=(rows // step,),
        in_specs=[pl.BlockSpec((step, depth), lambda i: (i, 0))] * n,
        out_specs=pl.BlockSpec((n, step, depth), lambda i: (0, i, 0)),
        out_shape=jax.ShapeDtypeStruct((n, rows, depth), parts[0].dtype),
        compiler_params=params(),
        cost_estimate=cost(0, 4 * n * rows * depth),
    )(*parts)


def whole_rows(stride, first, each):
    return lambda i, h: [(i, h * stride + first, each)]


def multiply(groups, own, other, at_k, where, before, each, halves, members, spread=True):
    held = members // 2
    last = before is not None and spread
    depth = groups[0][0][0].shape[-1]
    columns = own.shape[1]
    flat = [a for g in groups for a in g[0]]
    total_count = sum(g[1] for g in groups)
    rows = halves * each

    def body(where_ref, *refs):
        ins, w_refs = refs[: len(flat)], refs[len(flat) : len(flat) + 2]
        rest, (held_w, sems) = refs[len(flat) + 2 : -2], refs[-2:]
        total = rest[-1]
        copies = [
            [
                pltpu.make_async_copy(w_refs[side].at[at_k + k], held_w.at[k, side], sems.at[k, side])
                for side in range(2)
            ]
            for k in range(total_count)
        ]
        for pair in copies:
            for copy in pair:
                copy.start()
        starts = [h * before[0].shape[1] // halves + before[1] for h in range(halves)] if before is not None else []
        if last:
            for n in range(held):
                for h, start in enumerate(starts):
                    at = n * rows + h * each
                    total[at : at + each, :] = rest[0][n, start : start + each, :]
        k = 0
        for g, (_, count, pieces) in enumerate(groups):
            for i in range(count):
                taken = []
                for ref in ins[g * held : (g + 1) * held]:
                    for h in range(halves):
                        for slot, start, length in pieces(i, h):
                            span = slice(start, start + length)
                            taken.append(ref[slot, span, :] if len(ref.shape) == 3 else ref[span, :])
                stacked = jnp.concatenate(taken, axis=0)
                for side in range(2):
                    copies[k][side].wait()
                    product = lax.dot_general(
                        stacked, held_w[k, side], (((1,), (1,)), ((), ())), preferred_element_type=jnp.float32
                    )
                    span = slice(side * columns, (side + 1) * columns)
                    if last:
                        total[:, span] += product
                    else:
                        for n in range(held):
                            value = product[n * rows : (n + 1) * rows]
                            if k:
                                value = value + total[n, :, span]
                            elif before is not None:
                                value = value + jnp.concatenate([rest[0][n, at : at + each, span] for at in starts], axis=0)
                            total[n, :, span] = value
                k += 1
        if last:
            for n in range(held):
                for h in range(halves):
                    e = ((where_ref[1] ^ (2 * n)) * halves + h) ^ where_ref[0]
                    to, low = lax.div(e, 2 * halves), lax.rem(e, halves)
                    at = (n * halves + h) * each
                    for which in range(halves):

                        @pl.when(low == which)
                        def _(to=to, at=at, which=which):
                            for side in range(2):
                                rest[1 + side * halves + which][to] = total[
                                    at : at + each, side * columns : (side + 1) * columns
                                ]

    vmem, anywhere = pl.BlockSpec(memory_space=pltpu.VMEM), pl.BlockSpec(memory_space=pl.ANY)
    full = jax.ShapeDtypeStruct((held, rows, 2 * columns), jnp.float32)
    split = [jax.ShapeDtypeStruct((held, each, columns), jnp.float32)] * (2 * halves)
    return pl.pallas_call(
        body,
        in_specs=[pl.BlockSpec(memory_space=pltpu.SMEM)]
        + [vmem] * len(flat)
        + [anywhere] * 2
        + [vmem] * (before is not None),
        out_specs=[vmem] * (2 * halves) if last else vmem,
        out_shape=split if last else full,
        scratch_shapes=([pltpu.VMEM((held * rows, 2 * columns), jnp.float32)] if last else [])
        + [pltpu.VMEM((total_count, 2, columns, depth), jnp.bfloat16), pltpu.SemaphoreType.DMA((total_count, 2))],
        compiler_params=params(LIMIT),
        cost_estimate=cost(
            4 * held * rows * columns * depth * total_count, 2 * total_count * depth * (held * rows + 2 * columns)
        ),
    )(where, *flat, own, other, *((before[0],) if before is not None else ()))


def after(x, *done):
    return lax.optimization_barrier((x,) + done)[0] if done else x


def on_device(primal, adjoint_pencils, weights, pencil_map):
    rows_here, points = adjoint_pencils.shape
    tiles = lax.axis_size("space")
    members = lax.axis_size("snap")
    place, lane = lax.axis_index("space"), lax.axis_index("snap")
    where = jnp.stack([place, lane]).astype(jnp.int32)
    rows_out = rows_here * members // tiles
    halves = rows_here // rows_out
    adjoint = adjoint_pencils.reshape(halves, rows_out, points)
    half = tiles // 2
    middle = half + half // 2
    units = rows_out // ROWS
    rows_a = units // 2 * ROWS
    rows_b = max(1, 3 * units // 8) * ROWS
    rows_c = rows_out - rows_a - rows_b
    table = slots_of(pencil_map, place, tiles)

    tables = [pencil_map]

    def pack_rows(source, first, count, ks):
        packed = pack(source, tables[-1], where, first, count, ks, tiles)
        tables.extend(packed[len(ks) :])
        return dict(zip(ks, packed))

    def over_space(packed, ks, *done):
        return [xor_send(after(packed[k], *done), "space", k) for k in ks]

    def join(found):
        return found[0] if len(found) == 1 else merge(found)

    def across(block, *done):
        found, bit = [block], members // 2
        order = [0]
        while bit > 1:
            found = found + [xor_send(after(b, *done), "snap", bit) for b in found]
            order = order + [n ^ bit for n in order]
            bit //= 2
        return [found[order.index(n)] for n in sorted(order)]

    def swap_send(x, bit):
        pairs = [(i, i ^ (bit * members + 1)) for i in range(tiles * members)]
        return lax.ppermute(x, ("space", "snap"), pairs)

    same = (((lane * halves) ^ place) & halves) == 0

    class Sum:
        def __init__(self, parts, *done):
            self.mine, self.give = parts[:halves], parts[halves:]
            self.got = [
                (xor_send(after(self.mine[low], *done), "space", low), swap_send(after(self.give[low], *done), low))
                for low in range(1, halves)
            ]

        def swap(self, *done):
            self.swapped = xor_send(after(self.give[0], *done), "snap", 1)
            return self

        def finish(self, *done):
            own = sum([g[0] for g in self.got], self.mine[0])
            rest = sum([g[1] for g in self.got], self.swapped)
            zero, one = jnp.where(same, own, rest), jnp.where(same, rest, own)
            total = zero[0]
            self.last = []
            for hi in range(members // 2):
                for core, part in enumerate((zero, one)):
                    if hi or core:
                        self.last.append(xor_send(after(part[hi], *done), "space", halves * (core + 2 * hi)))
            return sum(self.last, total)

    near_a, near_b = list(range(2, 2 + (half - 2) // 2)), list(range(2 + (half - 2) // 2, half))
    low, high = list(range(half, middle)), list(range(middle, tiles))

    rows_bc = rows_b + rows_c
    start_low, rest_low = low[: len(low) // 2], low[len(low) // 2 :]
    early = 2 + len(near_a)

    packed_a = pack_rows(adjoint, 0, rows_a, start_low)
    packed_n = pack_rows(after(adjoint, packed_a[low[0]]), 0, rows_out, [0, 1])
    packed_na = pack_rows(after(adjoint, packed_n[0]), 0, rows_a, near_a)
    low_a = over_space(packed_a, start_low)
    near_1 = over_space(packed_n, [1])[0]
    got_na = over_space(packed_na, near_a)
    cross_0 = across(packed_n[0])
    own_1 = weigh(after(primal, packed_na[near_a[0]]), weights, table, 0, early, tiles)
    own_2 = weigh(after(primal, own_1), weights, table, early, tiles - early, tiles)
    packed_ar = pack_rows(after(adjoint, own_2), 0, rows_a, rest_low)
    packed_nr = pack_rows(after(adjoint, packed_ar[rest_low[0]]), rows_a, rows_bc, near_a)

    done = (*low_a, near_1, *got_na, cross_0[-1], packed_nr[near_a[0]])
    low_a = low_a + over_space(packed_ar, rest_low, *done)
    got_na = got_na + over_space(packed_nr, near_a, *done)
    cross_1 = across(near_1, *done)
    other_1 = xor_send(after(own_1, *done), "snap", 1)
    other_2 = xor_send(after(own_2, *done), "snap", 1)
    packed_nb = pack_rows(after(adjoint, *done), 0, rows_a, near_b)
    packed_ah = pack_rows(after(adjoint, packed_nb[near_b[0]]), 0, rows_a, high)
    packed_bc = pack_rows(after(adjoint, packed_ah[high[0]]), rows_a, rows_bc, low + near_b)
    packed_b = pack_rows(after(adjoint, packed_bc[low[0]]), rows_a, rows_b, high)
    packed_c = pack_rows(after(adjoint, packed_b[high[0]]), rows_a + rows_b, rows_c, high)

    done = (*low_a, *got_na, cross_1[-1], other_1, other_2, packed_c[high[0]])
    high_a = over_space(packed_ah, high, *done)
    got_nb = over_space(packed_nb, near_b, *done)
    cross_low_a = across(join(low_a), *done)
    cross_na = across(join(got_na), *done)

    done = (*high_a, *got_nb, cross_low_a[-1], cross_na[-1])
    low_bc = over_space(packed_bc, low, *done)
    got_nb_bc = over_space(packed_bc, near_b, *done)
    cross_nb = across(join(got_nb), *done)
    cross_high_a = across(join(high_a), *done)

    def two_runs(i, h):
        return [(i, h * rows_a, rows_a), (len(near_a) + i, h * rows_bc, rows_bc)]

    plain = whole_rows(rows_out, 0, rows_out)
    groups = [(cross_0, 1, plain), (cross_1, 1, plain), (cross_na, len(near_a), two_runs)]
    product = multiply(groups, own_1, after(other_1, *done), 0, where, None, rows_out, halves, members)

    done = (*low_bc, *got_nb_bc, cross_nb[-1], cross_high_a[-1], product)
    high_b = over_space(packed_b, high, *done)
    cross_low_bc = across(join(low_bc), *done)
    cross_nb_bc = across(join(got_nb_bc), *done)
    rows = whole_rows(rows_a, 0, rows_a)
    groups = [(cross_nb, len(near_b), rows), (cross_low_a, len(low), rows), (cross_high_a, len(high), rows)]
    pair_a = multiply(groups, own_2, other_2, 0, where, (product, 0), rows_a, halves, members)

    done = (*high_b, cross_low_bc[-1], cross_nb_bc[-1], pair_a[0])
    high_c = over_space(packed_c, high, *done)
    cross_high_b = across(join(high_b), *done)
    sum_a = Sum(pair_a, *done)
    rows = whole_rows(rows_bc, 0, rows_bc)
    groups = [(cross_nb_bc, len(near_b), rows), (cross_low_bc, len(low), rows)]
    first_high = len(near_b) + len(low)
    product_bc = multiply(
        groups, own_2, after(other_2, *done), 0, where, (product, rows_a), rows_bc, halves, members, False
    )

    done = (*high_c, cross_high_b[-1], *[g for pair in sum_a.got for g in pair], product_bc)
    cross_high_c = across(join(high_c), *done)
    total_a = sum_a.swap(*done).finish()
    groups = [(cross_high_b, len(high), whole_rows(rows_b, 0, rows_b))]
    pair_b = multiply(groups, own_2, after(other_2, *done), first_high, where, (product_bc, 0), rows_b, halves, members)
    sum_b = Sum(pair_b, sum_a.swapped).swap()
    groups = [(cross_high_c, len(high), whole_rows(rows_c, 0, rows_c))]
    pair_c = multiply(
        groups, own_2, after(other_2, *sum_a.last), first_high, where, (product_bc, rows_b), rows_c, halves, members
    )
    sum_c = Sum(pair_c).swap()
    return jnp.concatenate([total_a, sum_b.finish(), sum_c.finish()], axis=0)


def solution(mesh):
    placed = (P("snap", "space"), P("snap", "space"), P("space"), P())
    return jax.shard_map(
        on_device, mesh=mesh, in_specs=placed, out_specs=P("space", "snap"), check_vma=False
    )
```

```python
import jax
import jax.numpy as jnp
from jax import lax
from jax.experimental import pallas as pl
from jax.experimental.pallas import tpu as pltpu
from jax.sharding import PartitionSpec as P

PEN_LEN = 128
ROWS = 16
COST_SCALE = 1
LIMIT = 50


def xor_send(x, axis, k):
    n = lax.axis_size(axis)
    return lax.ppermute(x, axis, [(i, i ^ k) for i in range(n)])


def params(mebibytes=8):
    return pltpu.CompilerParams(vmem_limit_bytes=mebibytes * 1024 * 1024)


def cost(flops, nbytes):
    return pl.CostEstimate(flops=flops // COST_SCALE, bytes_accessed=nbytes // COST_SCALE, transcendentals=0)


def pack(adjoint, table, where, jobs, tiles):
    halves, _, points = adjoint.shape
    pen_dev = points // PEN_LEN
    share = pen_dev // tiles
    build = table.shape[0] != pen_dev
    magic = (1 << 20) // pen_dev + 1
    exact = all(x * magic >> 20 == x // pen_dev for x in range(tiles * pen_dev))

    def body(table_ref, where_ref, in_ref, *refs):
        outs = refs[: len(jobs)]
        if build:
            made, seen = refs[len(jobs) :]
            place = where_ref[0]
            for k in range(tiles):
                seen[k] = 0

            def enter(q, carry):
                slot = table_ref[place * pen_dev + q]
                k = (slot * magic >> 20 if exact else lax.div(slot, pen_dev)) ^ place
                t = seen[k]
                seen[k] = t + 1
                made[k * share + t] = q
                return carry

            lax.fori_loop(0, pen_dev, enter, 0, unroll=8)
        else:
            made = table_ref
        for o, (k, first, count) in enumerate(jobs):
            for t in range(share):
                start = pl.multiple_of(made[k * share + t] * PEN_LEN, PEN_LEN)
                for h in range(halves):
                    outs[o][h * count : (h + 1) * count, t * PEN_LEN : (t + 1) * PEN_LEN] = in_ref[
                        h, first : first + count, pl.ds(start, PEN_LEN)
                    ]

    smem, vmem = pl.BlockSpec(memory_space=pltpu.SMEM), pl.BlockSpec(memory_space=pltpu.VMEM)
    return pl.pallas_call(
        body,
        in_specs=[smem, smem, vmem],
        out_specs=[vmem] * len(jobs) + [smem] * build,
        out_shape=[jax.ShapeDtypeStruct((halves * count, share * PEN_LEN), jnp.bfloat16) for _, _, count in jobs]
        + [jax.ShapeDtypeStruct((pen_dev,), jnp.int32)] * build,
        scratch_shapes=[pltpu.SMEM((tiles,), jnp.int32)] * build,
        compiler_params=params(),
        cost_estimate=cost(0, 4 * halves * sum(count for _, _, count in jobs) * share * PEN_LEN),
    )(table, where, adjoint)


def slots_of(pencil_map, place, tiles):
    pen_dev = pencil_map.shape[0] // tiles
    share = pen_dev // tiles
    local = pencil_map.reshape(tiles, pen_dev) - place * pen_dev
    here = (local >= 0) & (local < pen_dev)
    q = jnp.arange(pen_dev)
    rank = jnp.sum(here[:, None, :] & (q[None, None, :] < q[None, :, None]), axis=2)
    match = here[:, None, :] & (rank[:, None, :] == jnp.arange(share)[None, :, None])
    table = jnp.sum(jnp.where(match, local[:, None, :], 0), axis=2)
    order = jnp.arange(tiles) ^ place
    picked = jnp.sum(jnp.where(order[:, None, None] == jnp.arange(tiles)[None, :, None], table[None], 0), axis=1)
    return picked.reshape(pen_dev).astype(jnp.int32)


def weigh(primal, weights, table, first, count, tiles):
    rows, points = primal.shape
    share = points // PEN_LEN // tiles
    step = 64 if rows % 64 == 0 else rows

    def body(table_ref, in_ref, w_ref, out):
        for k in range(count):
            for t in range(share):
                start = pl.multiple_of(table_ref[(first + k) * share + t] * PEN_LEN, PEN_LEN)
                scale = w_ref[:, pl.ds(start, PEN_LEN)]
                for i in range(0, rows, step):
                    tile = in_ref[i : i + step, pl.ds(start, PEN_LEN)].astype(jnp.float32) * scale
                    out[k, i : i + step, t * PEN_LEN : (t + 1) * PEN_LEN] = tile.astype(jnp.bfloat16)

    vmem = pl.BlockSpec(memory_space=pltpu.VMEM)
    return pl.pallas_call(
        body,
        in_specs=[pl.BlockSpec(memory_space=pltpu.SMEM), vmem, vmem],
        out_specs=vmem,
        out_shape=jax.ShapeDtypeStruct((count, rows, share * PEN_LEN), jnp.bfloat16),
        compiler_params=params(),
        cost_estimate=cost(rows * points // 2, 3 * rows * points),
    )(table, primal, weights.reshape(1, points))


def merge(parts):
    n = len(parts)
    rows, depth = parts[0].shape
    step = rows // 2 if rows % (2 * ROWS) == 0 else rows

    def body(*refs):
        for i in range(n):
            refs[n][i] = refs[i][...]

    return pl.pallas_call(
        body,
        grid=(rows // step,),
        in_specs=[pl.BlockSpec((step, depth), lambda i: (i, 0))] * n,
        out_specs=pl.BlockSpec((n, step, depth), lambda i: (0, i, 0)),
        out_shape=jax.ShapeDtypeStruct((n, rows, depth), parts[0].dtype),
        compiler_params=params(),
        cost_estimate=cost(0, 4 * n * rows * depth),
    )(*parts)


def whole_rows(stride, first, each):
    return lambda i, h: [(i, h * stride + first, each)]


def multiply(groups, own, other, at_k, where, before, each, halves, members, spread=True):
    held = members // 2
    last = before is not None and spread
    depth = groups[0][0][0].shape[-1]
    columns = own.shape[1]
    flat = [a for g in groups for a in g[0]]
    total_count = sum(g[1] for g in groups)
    rows = halves * each

    def body(where_ref, *refs):
        ins, w_refs = refs[: len(flat)], refs[len(flat) : len(flat) + 2]
        rest, (held_w, sems) = refs[len(flat) + 2 : -2], refs[-2:]
        total = rest[-1]
        copies = [
            [
                pltpu.make_async_copy(w_refs[side].at[at_k + k], held_w.at[k, side], sems.at[k, side])
                for side in range(2)
            ]
            for k in range(total_count)
        ]
        for pair in copies:
            for copy in pair:
                copy.start()
        starts = [h * before[0].shape[1] // halves + before[1] for h in range(halves)] if before is not None else []
        if last:
            for n in range(held):
                for h, start in enumerate(starts):
                    at = n * rows + h * each
                    total[at : at + each, :] = rest[0][n, start : start + each, :]
        k = 0
        for g, (_, count, pieces) in enumerate(groups):
            for i in range(count):
                taken = []
                for ref in ins[g * held : (g + 1) * held]:
                    for h in range(halves):
                        for slot, start, length in pieces(i, h):
                            span = slice(start, start + length)
                            taken.append(ref[slot, span, :] if len(ref.shape) == 3 else ref[span, :])
                stacked = jnp.concatenate(taken, axis=0)
                for side in range(2):
                    copies[k][side].wait()
                    product = lax.dot_general(
                        stacked, held_w[k, side], (((1,), (1,)), ((), ())), preferred_element_type=jnp.float32
                    )
                    span = slice(side * columns, (side + 1) * columns)
                    if last:
                        total[:, span] += product
                    else:
                        for n in range(held):
                            value = product[n * rows : (n + 1) * rows]
                            if k:
                                value = value + total[n, :, span]
                            elif before is not None:
                                value = value + jnp.concatenate([rest[0][n, at : at + each, span] for at in starts], axis=0)
                            total[n, :, span] = value
                k += 1
        if last:
            for n in range(held):
                for h in range(halves):
                    e = ((where_ref[1] ^ (2 * n)) * halves + h) ^ where_ref[0]
                    to, low = lax.div(e, 2 * halves), lax.rem(e, halves)
                    at = (n * halves + h) * each
                    for which in range(halves):

                        @pl.when(low == which)
                        def _(to=to, at=at, which=which):
                            for side in range(2):
                                rest[1 + side * halves + which][to] = total[
                                    at : at + each, side * columns : (side + 1) * columns
                                ]

    vmem, anywhere = pl.BlockSpec(memory_space=pltpu.VMEM), pl.BlockSpec(memory_space=pl.ANY)
    full = jax.ShapeDtypeStruct((held, rows, 2 * columns), jnp.float32)
    split = [jax.ShapeDtypeStruct((held, each, columns), jnp.float32)] * (2 * halves)
    return pl.pallas_call(
        body,
        in_specs=[pl.BlockSpec(memory_space=pltpu.SMEM)]
        + [vmem] * len(flat)
        + [anywhere] * 2
        + [vmem] * (before is not None),
        out_specs=[vmem] * (2 * halves) if last else vmem,
        out_shape=split if last else full,
        scratch_shapes=([pltpu.VMEM((held * rows, 2 * columns), jnp.float32)] if last else [])
        + [pltpu.VMEM((total_count, 2, columns, depth), jnp.bfloat16), pltpu.SemaphoreType.DMA((total_count, 2))],
        compiler_params=params(LIMIT),
        cost_estimate=cost(
            4 * held * rows * columns * depth * total_count, 2 * total_count * depth * (held * rows + 2 * columns)
        ),
    )(where, *flat, own, other, *((before[0],) if before is not None else ()))


def after(x, *done):
    return lax.optimization_barrier((x,) + done)[0] if done else x


def on_device(primal, adjoint_pencils, weights, pencil_map):
    rows_here, points = adjoint_pencils.shape
    tiles = lax.axis_size("space")
    members = lax.axis_size("snap")
    place, lane = lax.axis_index("space"), lax.axis_index("snap")
    where = jnp.stack([place, lane]).astype(jnp.int32)
    rows_out = rows_here * members // tiles
    halves = rows_here // rows_out
    adjoint = adjoint_pencils.reshape(halves, rows_out, points)
    half = tiles // 2
    middle = half + half // 2
    units = rows_out // ROWS
    rows_a = units // 2 * ROWS
    rows_b = max(1, 3 * units // 8) * ROWS
    rows_c = rows_out - rows_a - rows_b
    table = slots_of(pencil_map, place, tiles)

    tables = [pencil_map]

    def pack_rows(source, *runs):
        jobs = [(k, first, count) for first, count, ks in runs for k in ks]
        packed = pack(source, tables[-1], where, jobs, tiles)
        tables.extend(packed[len(jobs) :])
        out = [dict(zip(ks, packed[sum(len(r[2]) for r in runs[:i]) :])) for i, (_, _, ks) in enumerate(runs)]
        return out[0] if len(out) == 1 else out

    def over_space(packed, ks, *done):
        return [xor_send(after(packed[k], *done), "space", k) for k in ks]

    def join(found):
        return found[0] if len(found) == 1 else merge(found)

    def across(block, *done):
        found, bit = [block], members // 2
        order = [0]
        while bit > 1:
            found = found + [xor_send(after(b, *done), "snap", bit) for b in found]
            order = order + [n ^ bit for n in order]
            bit //= 2
        return [found[order.index(n)] for n in sorted(order)]

    def swap_send(x, bit):
        pairs = [(i, i ^ (bit * members + 1)) for i in range(tiles * members)]
        return lax.ppermute(x, ("space", "snap"), pairs)

    same = (((lane * halves) ^ place) & halves) == 0

    class Sum:
        def __init__(self, parts, *done):
            self.mine, self.give = parts[:halves], parts[halves:]
            self.got = [
                (xor_send(after(self.mine[low], *done), "space", low), swap_send(after(self.give[low], *done), low))
                for low in range(1, halves)
            ]

        def swap(self, *done):
            self.swapped = xor_send(after(self.give[0], *done), "snap", 1)
            return self

        def finish(self, *done):
            own = sum([g[0] for g in self.got], self.mine[0])
            rest = sum([g[1] for g in self.got], self.swapped)
            zero, one = jnp.where(same, own, rest), jnp.where(same, rest, own)
            total = zero[0]
            self.last = []
            for hi in range(members // 2):
                for core, part in enumerate((zero, one)):
                    if hi or core:
                        self.last.append(xor_send(after(part[hi], *done), "space", halves * (core + 2 * hi)))
            return sum(self.last, total)

    near_a, near_b = list(range(2, 2 + (half - 2) // 2)), list(range(2 + (half - 2) // 2, half))
    low, high = list(range(half, middle)), list(range(middle, tiles))

    rows_bc = rows_b + rows_c
    start_low, rest_low = low[: len(low) // 2], low[len(low) // 2 :]
    early = 2 + len(near_a)

    packed_n, packed_a, packed_na = pack_rows(
        adjoint, (0, rows_out, [0, 1]), (0, rows_a, start_low), (0, rows_a, near_a)
    )
    low_a = over_space(packed_a, start_low)
    near_1 = over_space(packed_n, [1])[0]
    got_na = over_space(packed_na, near_a)
    cross_0 = across(packed_n[0])
    own_1 = weigh(after(primal, packed_na[near_a[0]]), weights, table, 0, early, tiles)
    own_2 = weigh(after(primal, own_1), weights, table, early, tiles - early, tiles)
    packed_ar = pack_rows(after(adjoint, own_2), (0, rows_a, rest_low))
    packed_nr = pack_rows(after(adjoint, packed_ar[rest_low[0]]), (rows_a, rows_bc, near_a))

    done = (*low_a, near_1, *got_na, cross_0[-1], packed_nr[near_a[0]])
    low_a = low_a + over_space(packed_ar, rest_low, *done)
    got_na = got_na + over_space(packed_nr, near_a, *done)
    cross_1 = across(near_1, *done)
    other_1 = xor_send(after(own_1, *done), "snap", 1)
    other_2 = xor_send(after(own_2, *done), "snap", 1)
    packed_nb = pack_rows(after(adjoint, *done), (0, rows_a, near_b))
    packed_ah = pack_rows(after(adjoint, packed_nb[near_b[0]]), (0, rows_a, high))
    packed_bc = pack_rows(after(adjoint, packed_ah[high[0]]), (rows_a, rows_bc, low + near_b))
    packed_b = pack_rows(after(adjoint, packed_bc[low[0]]), (rows_a, rows_b, high))
    packed_c = pack_rows(after(adjoint, packed_b[high[0]]), (rows_a + rows_b, rows_c, high))

    done = (*low_a, *got_na, cross_1[-1], other_1, other_2, packed_c[high[0]])
    high_a = over_space(packed_ah, high, *done)
    got_nb = over_space(packed_nb, near_b, *done)
    cross_low_a = across(join(low_a), *done)
    cross_na = across(join(got_na), *done)

    done = (*high_a, *got_nb, cross_low_a[-1], cross_na[-1])
    low_bc = over_space(packed_bc, low, *done)
    got_nb_bc = over_space(packed_bc, near_b, *done)
    cross_nb = across(join(got_nb), *done)
    cross_high_a = across(join(high_a), *done)

    def two_runs(i, h):
        return [(i, h * rows_a, rows_a), (len(near_a) + i, h * rows_bc, rows_bc)]

    plain = whole_rows(rows_out, 0, rows_out)
    groups = [(cross_0, 1, plain), (cross_1, 1, plain), (cross_na, len(near_a), two_runs)]
    product = multiply(groups, own_1, after(other_1, *done), 0, where, None, rows_out, halves, members)

    done = (*got_nb_bc, *low_bc, cross_nb[-1], cross_high_a[-1], product)
    high_b = over_space(packed_b, high, *done)
    cross_low_bc = across(join(low_bc), *done)
    cross_nb_bc = across(join(got_nb_bc), *done)
    rows = whole_rows(rows_a, 0, rows_a)
    groups = [(cross_nb, len(near_b), rows), (cross_low_a, len(low), rows), (cross_high_a, len(high), rows)]
    pair_a = multiply(groups, own_2, other_2, 0, where, (product, 0), rows_a, halves, members)

    done = (*high_b, cross_low_bc[-1], cross_nb_bc[-1], pair_a[0])
    high_c = over_space(packed_c, high, *done)
    cross_high_b = across(join(high_b), *done)
    sum_a = Sum(pair_a, *done)
    rows = whole_rows(rows_bc, 0, rows_bc)
    groups = [(cross_nb_bc, len(near_b), rows), (cross_low_bc, len(low), rows)]
    first_high = len(near_b) + len(low)
    product_bc = multiply(
        groups, own_2, after(other_2, *done), 0, where, (product, rows_a), rows_bc, halves, members, False
    )

    done = (*high_c, cross_high_b[-1], *[g for pair in sum_a.got for g in pair], product_bc)
    cross_high_c = across(join(high_c), *done)
    total_a = sum_a.swap(*done).finish()
    groups = [(cross_high_b, len(high), whole_rows(rows_b, 0, rows_b))]
    pair_b = multiply(groups, own_2, after(other_2, *done), first_high, where, (product_bc, 0), rows_b, halves, members)
    sum_b = Sum(pair_b, sum_a.swapped).swap()
    groups = [(cross_high_c, len(high), whole_rows(rows_c, 0, rows_c))]
    pair_c = multiply(
        groups, own_2, after(other_2, *sum_a.last[::2]), first_high, where, (product_bc, rows_b), rows_c, halves, members
    )
    sum_c = Sum(pair_c).swap()
    return jnp.concatenate([total_a, sum_b.finish(), sum_c.finish()], axis=0)


def solution(mesh):
    placed = (P("snap", "space"), P("snap", "space"), P("space"), P())
    return jax.shard_map(
        on_device, mesh=mesh, in_specs=placed, out_specs=P("space", "snap"), check_vma=False
    )
```

```python
import jax
import jax.numpy as jnp
from jax import lax
from jax.experimental import pallas as pl
from jax.experimental.pallas import tpu as pltpu
from jax.sharding import PartitionSpec as P

PEN_LEN = 128
ROWS = 16
COST_SCALE = 1
LIMIT = 50


def xor_send(x, axis, k):
    n = lax.axis_size(axis)
    return lax.ppermute(x, axis, [(i, i ^ k) for i in range(n)])


def params(mebibytes=3):
    return pltpu.CompilerParams(vmem_limit_bytes=mebibytes * 1024 * 1024)


def cost(flops, nbytes):
    return pl.CostEstimate(flops=flops // COST_SCALE, bytes_accessed=nbytes // COST_SCALE, transcendentals=0)


def pack(adjoint, table, where, jobs, tiles):
    halves, _, points = adjoint.shape
    pen_dev = points // PEN_LEN
    share = pen_dev // tiles
    build = table.shape[0] != pen_dev
    magic = (1 << 20) // pen_dev + 1
    exact = all(x * magic >> 20 == x // pen_dev for x in range(tiles * pen_dev))

    def body(table_ref, where_ref, in_ref, *refs):
        outs = refs[: len(jobs)]
        if build:
            made, seen = refs[len(jobs) :]
            place = where_ref[0]
            for k in range(tiles):
                seen[k] = 0

            def enter(q, carry):
                slot = table_ref[place * pen_dev + q]
                k = (slot * magic >> 20 if exact else lax.div(slot, pen_dev)) ^ place
                t = seen[k]
                seen[k] = t + 1
                made[k * share + t] = q
                return carry

            lax.fori_loop(0, pen_dev, enter, 0, unroll=8)
        else:
            made = table_ref
        for o, (k, first, count) in enumerate(jobs):
            for t in range(share):
                start = pl.multiple_of(made[k * share + t] * PEN_LEN, PEN_LEN)
                for h in range(halves):
                    outs[o][h * count : (h + 1) * count, t * PEN_LEN : (t + 1) * PEN_LEN] = in_ref[
                        h, first : first + count, pl.ds(start, PEN_LEN)
                    ]

    smem, vmem = pl.BlockSpec(memory_space=pltpu.SMEM), pl.BlockSpec(memory_space=pltpu.VMEM)
    return pl.pallas_call(
        body,
        in_specs=[smem, smem, vmem],
        out_specs=[vmem] * len(jobs) + [smem] * build,
        out_shape=[jax.ShapeDtypeStruct((halves * count, share * PEN_LEN), jnp.bfloat16) for _, _, count in jobs]
        + [jax.ShapeDtypeStruct((pen_dev,), jnp.int32)] * build,
        scratch_shapes=[pltpu.SMEM((tiles,), jnp.int32)] * build,
        compiler_params=params(),
        cost_estimate=cost(0, 4 * halves * sum(count for _, _, count in jobs) * share * PEN_LEN),
    )(table, where, adjoint)


def slots_of(pencil_map, place, tiles):
    pen_dev = pencil_map.shape[0] // tiles
    share = pen_dev // tiles
    local = pencil_map.reshape(tiles, pen_dev) - place * pen_dev
    here = (local >= 0) & (local < pen_dev)
    q = jnp.arange(pen_dev)
    rank = jnp.sum(here[:, None, :] & (q[None, None, :] < q[None, :, None]), axis=2)
    match = here[:, None, :] & (rank[:, None, :] == jnp.arange(share)[None, :, None])
    table = jnp.sum(jnp.where(match, local[:, None, :], 0), axis=2)
    order = jnp.arange(tiles) ^ place
    picked = jnp.sum(jnp.where(order[:, None, None] == jnp.arange(tiles)[None, :, None], table[None], 0), axis=1)
    return picked.reshape(pen_dev).astype(jnp.int32)


def weigh(primal, weights, table, first, count, tiles):
    rows, points = primal.shape
    share = points // PEN_LEN // tiles
    step = 64 if rows % 64 == 0 else rows

    def body(table_ref, in_ref, w_ref, out):
        for k in range(count):
            for t in range(share):
                start = pl.multiple_of(table_ref[(first + k) * share + t] * PEN_LEN, PEN_LEN)
                scale = w_ref[:, pl.ds(start, PEN_LEN)]
                for i in range(0, rows, step):
                    tile = in_ref[i : i + step, pl.ds(start, PEN_LEN)].astype(jnp.float32) * scale
                    out[k, i : i + step, t * PEN_LEN : (t + 1) * PEN_LEN] = tile.astype(jnp.bfloat16)

    vmem = pl.BlockSpec(memory_space=pltpu.VMEM)
    return pl.pallas_call(
        body,
        in_specs=[pl.BlockSpec(memory_space=pltpu.SMEM), vmem, vmem],
        out_specs=vmem,
        out_shape=jax.ShapeDtypeStruct((count, rows, share * PEN_LEN), jnp.bfloat16),
        compiler_params=params(),
        cost_estimate=cost(rows * points // 2, 3 * rows * points),
    )(table, primal, weights.reshape(1, points))


def merge(parts):
    n = len(parts)
    rows, depth = parts[0].shape
    step = rows // 2 if rows % (2 * ROWS) == 0 else rows

    def body(*refs):
        for i in range(n):
            refs[n][i] = refs[i][...]

    return pl.pallas_call(
        body,
        grid=(rows // step,),
        in_specs=[pl.BlockSpec((step, depth), lambda i: (i, 0))] * n,
        out_specs=pl.BlockSpec((n, step, depth), lambda i: (0, i, 0)),
        out_shape=jax.ShapeDtypeStruct((n, rows, depth), parts[0].dtype),
        compiler_params=params(),
        cost_estimate=cost(0, 4 * n * rows * depth),
    )(*parts)


def whole_rows(stride, first, each):
    return lambda i, h: [(i, h * stride + first, each)]


def multiply(groups, own, other, at_k, where, before, each, halves, members, spread=True):
    held = members // 2
    last = before is not None and spread
    depth = groups[0][0][0].shape[-1]
    columns = own.shape[1]
    flat = [a for g in groups for a in g[0]]
    total_count = sum(g[1] for g in groups)
    rows = halves * each

    def body(where_ref, *refs):
        ins, w_refs = refs[: len(flat)], refs[len(flat) : len(flat) + 2]
        rest, (held_w, sems) = refs[len(flat) + 2 : -2], refs[-2:]
        total = rest[-1]
        copies = [
            [
                pltpu.make_async_copy(w_refs[side].at[at_k + k], held_w.at[k, side], sems.at[k, side])
                for side in range(2)
            ]
            for k in range(total_count)
        ]
        for pair in copies:
            for copy in pair:
                copy.start()
        starts = [h * before[0].shape[1] // halves + before[1] for h in range(halves)] if before is not None else []
        if last:
            for n in range(held):
                for h, start in enumerate(starts):
                    at = n * rows + h * each
                    total[at : at + each, :] = rest[0][n, start : start + each, :]
        k = 0
        for g, (_, count, pieces) in enumerate(groups):
            for i in range(count):
                taken = []
                for ref in ins[g * held : (g + 1) * held]:
                    for h in range(halves):
                        for slot, start, length in pieces(i, h):
                            span = slice(start, start + length)
                            taken.append(ref[slot, span, :] if len(ref.shape) == 3 else ref[span, :])
                stacked = jnp.concatenate(taken, axis=0)
                for side in range(2):
                    copies[k][side].wait()
                    product = lax.dot_general(
                        stacked, held_w[k, side], (((1,), (1,)), ((), ())), preferred_element_type=jnp.float32
                    )
                    span = slice(side * columns, (side + 1) * columns)
                    if last:
                        total[:, span] += product
                    else:
                        for n in range(held):
                            value = product[n * rows : (n + 1) * rows]
                            if k:
                                value = value + total[n, :, span]
                            elif before is not None:
                                value = value + jnp.concatenate([rest[0][n, at : at + each, span] for at in starts], axis=0)
                            total[n, :, span] = value
                k += 1
        if last:
            for n in range(held):
                for h in range(halves):
                    e = ((where_ref[1] ^ (2 * n)) * halves + h) ^ where_ref[0]
                    to, low = lax.div(e, 2 * halves), lax.rem(e, halves)
                    at = (n * halves + h) * each
                    for which in range(halves):

                        @pl.when(low == which)
                        def _(to=to, at=at, which=which):
                            for side in range(2):
                                rest[1 + side * halves + which][to] = total[
                                    at : at + each, side * columns : (side + 1) * columns
                                ]

    vmem, anywhere = pl.BlockSpec(memory_space=pltpu.VMEM), pl.BlockSpec(memory_space=pl.ANY)
    full = jax.ShapeDtypeStruct((held, rows, 2 * columns), jnp.float32)
    split = [jax.ShapeDtypeStruct((held, each, columns), jnp.float32)] * (2 * halves)
    return pl.pallas_call(
        body,
        in_specs=[pl.BlockSpec(memory_space=pltpu.SMEM)]
        + [vmem] * len(flat)
        + [anywhere] * 2
        + [vmem] * (before is not None),
        out_specs=[vmem] * (2 * halves) if last else vmem,
        out_shape=split if last else full,
        scratch_shapes=([pltpu.VMEM((held * rows, 2 * columns), jnp.float32)] if last else [])
        + [pltpu.VMEM((total_count, 2, columns, depth), jnp.bfloat16), pltpu.SemaphoreType.DMA((total_count, 2))],
        compiler_params=params(LIMIT),
        cost_estimate=cost(
            4 * held * rows * columns * depth * total_count, 2 * total_count * depth * (held * rows + 2 * columns)
        ),
    )(where, *flat, own, other, *((before[0],) if before is not None else ()))


def after(x, *done):
    return lax.optimization_barrier((x,) + done)[0] if done else x


def on_device(primal, adjoint_pencils, weights, pencil_map):
    rows_here, points = adjoint_pencils.shape
    tiles = lax.axis_size("space")
    members = lax.axis_size("snap")
    place, lane = lax.axis_index("space"), lax.axis_index("snap")
    where = jnp.stack([place, lane]).astype(jnp.int32)
    rows_out = rows_here * members // tiles
    halves = rows_here // rows_out
    adjoint = adjoint_pencils.reshape(halves, rows_out, points)
    half = tiles // 2
    middle = half + half // 2
    units = rows_out // ROWS
    rows_a = units // 2 * ROWS
    rows_b = max(1, 3 * units // 8) * ROWS
    rows_c = rows_out - rows_a - rows_b
    table = slots_of(pencil_map, place, tiles)

    tables = [pencil_map]

    def pack_rows(source, *runs):
        jobs = [(k, first, count) for first, count, ks in runs for k in ks]
        packed = pack(source, tables[-1], where, jobs, tiles)
        tables.extend(packed[len(jobs) :])
        out = [dict(zip(ks, packed[sum(len(r[2]) for r in runs[:i]) :])) for i, (_, _, ks) in enumerate(runs)]
        return out[0] if len(out) == 1 else out

    def over_space(packed, ks, *done):
        return [xor_send(after(packed[k], *done), "space", k) for k in ks]

    def join(found):
        return found[0] if len(found) == 1 else merge(found)

    def across(block, *done):
        found, bit = [block], members // 2
        order = [0]
        while bit > 1:
            found = found + [xor_send(after(b, *done), "snap", bit) for b in found]
            order = order + [n ^ bit for n in order]
            bit //= 2
        return [found[order.index(n)] for n in sorted(order)]

    def swap_send(x, bit):
        pairs = [(i, i ^ (bit * members + 1)) for i in range(tiles * members)]
        return lax.ppermute(x, ("space", "snap"), pairs)

    same = (((lane * halves) ^ place) & halves) == 0

    class Sum:
        def __init__(self, parts):
            self.mine, self.give = parts[:halves], parts[halves:]

        def halve_mine(self, *done):
            self.got = [xor_send(after(self.mine[low], *done), "space", low) for low in range(1, halves)]
            return self

        def halve_give(self, *done):
            self.got_give = [swap_send(after(self.give[low], *done), low) for low in range(1, halves)]
            return self

        def swap(self, *done):
            self.swapped = xor_send(after(self.give[0], *done), "snap", 1)
            return self

        def finish(self, *done):
            own = sum(self.got, self.mine[0])
            rest = sum(self.got_give, self.swapped)
            zero, one = jnp.where(same, own, rest), jnp.where(same, rest, own)
            total = zero[0]
            self.last = []
            for hi in range(members // 2):
                for core, part in enumerate((zero, one)):
                    if hi or core:
                        self.last.append(xor_send(after(part[hi], *done), "space", halves * (core + 2 * hi)))
            return sum(self.last, total)

    near_a, near_b = list(range(2, 2 + (half - 2) // 2)), list(range(2 + (half - 2) // 2, half))
    low, high = list(range(half, middle)), list(range(middle, tiles))

    rows_bc = rows_b + rows_c
    start_low, rest_low = low[: len(low) // 2], low[len(low) // 2 :]
    early = 2 + len(near_a)

    packed_n, packed_a, packed_na = pack_rows(
        adjoint, (0, rows_out, [0, 1]), (0, rows_a, start_low), (0, rows_a, near_a)
    )
    low_a = over_space(packed_a, start_low)
    near_1 = over_space(packed_n, [1])[0]
    got_na = over_space(packed_na, near_a)
    cross_0 = across(packed_n[0])
    own_1 = weigh(after(primal, packed_na[near_a[0]]), weights, table, 0, early, tiles)
    own_2 = weigh(after(primal, own_1), weights, table, early, tiles - early, tiles)
    packed_ar = pack_rows(after(adjoint, own_2), (0, rows_a, rest_low))
    packed_nr = pack_rows(after(adjoint, packed_ar[rest_low[0]]), (rows_a, rows_bc, near_a))

    done = (*low_a, near_1, *got_na, cross_0[-1], packed_nr[near_a[0]])
    low_a = low_a + over_space(packed_ar, rest_low, *done)
    got_na = got_na + over_space(packed_nr, near_a, *done)
    cross_1 = across(near_1, *done)
    other_1 = xor_send(after(own_1, *done), "snap", 1)
    other_2 = xor_send(after(own_2, *done), "snap", 1)
    packed_nb = pack_rows(after(adjoint, *done), (0, rows_a, near_b))
    packed_ah = pack_rows(after(adjoint, packed_nb[near_b[0]]), (0, rows_a, high))
    packed_bc = pack_rows(after(adjoint, packed_ah[high[0]]), (rows_a, rows_bc, low + near_b))
    packed_b = pack_rows(after(adjoint, packed_bc[low[0]]), (rows_a, rows_b, high))
    packed_c = pack_rows(after(adjoint, packed_b[high[0]]), (rows_a + rows_b, rows_c, high))

    done = (*low_a, *got_na, cross_1[-1], other_1, other_2, packed_c[high[0]])
    high_a = over_space(packed_ah, high, *done)
    got_nb = over_space(packed_nb, near_b, *done)
    cross_low_a = across(join(low_a), *done)
    cross_na = across(join(got_na), *done)

    done = (*high_a, *got_nb, cross_low_a[-1], cross_na[-1])
    low_bc = over_space(packed_bc, low, *done)
    got_nb_bc = over_space(packed_bc, near_b, *done)
    cross_nb = across(join(got_nb), *done)
    cross_high_a = across(join(high_a), *done)

    def two_runs(i, h):
        return [(i, h * rows_a, rows_a), (len(near_a) + i, h * rows_bc, rows_bc)]

    plain = whole_rows(rows_out, 0, rows_out)
    groups = [(cross_0, 1, plain), (cross_1, 1, plain), (cross_na, len(near_a), two_runs)]
    product = multiply(groups, own_1, after(other_1, *done), 0, where, None, rows_out, halves, members)

    done = (*got_nb_bc, *low_bc, cross_nb[-1], cross_high_a[-1], product)
    high_b = over_space(packed_b, high, *done)
    cross_low_bc = across(join(low_bc), *done)
    cross_nb_bc = across(join(got_nb_bc), *done)
    rows = whole_rows(rows_a, 0, rows_a)
    groups = [(cross_nb, len(near_b), rows), (cross_low_a, len(low), rows), (cross_high_a, len(high), rows)]
    pair_a = multiply(groups, own_2, other_2, 0, where, (product, 0), rows_a, halves, members)

    sum_a = Sum(pair_a).halve_mine()

    done = (*high_b, cross_low_bc[-1], cross_nb_bc[-1], pair_a[0], *sum_a.got)
    high_c = over_space(packed_c, high, *done)
    cross_high_b = across(join(high_b), *done)
    sum_a.halve_give(*done).swap(*done)
    rows = whole_rows(rows_bc, 0, rows_bc)
    groups = [(cross_nb_bc, len(near_b), rows), (cross_low_bc, len(low), rows)]
    first_high = len(near_b) + len(low)
    product_bc = multiply(
        groups, own_2, after(other_2, *done), 0, where, (product, rows_a), rows_bc, halves, members, False
    )

    done = (*high_c, cross_high_b[-1], *sum_a.got_give, sum_a.swapped, product_bc)
    cross_high_c = across(join(high_c), *done)
    total_a = sum_a.finish(*done)
    groups = [(cross_high_b, len(high), whole_rows(rows_b, 0, rows_b))]
    pair_b = multiply(groups, own_2, after(other_2, *done), first_high, where, (product_bc, 0), rows_b, halves, members)
    crossed = cross_high_c[-1]
    sum_b = Sum(pair_b).halve_mine(cross_high_c[-1]).halve_give(cross_high_c[-1]).swap(cross_high_c[-1])
    groups = [(cross_high_c, len(high), whole_rows(rows_c, 0, rows_c))]
    pair_c = multiply(
        groups, own_2, after(other_2, *sum_a.last[::2], sum_b.swapped), first_high, where, (product_bc, rows_b), rows_c, halves, members
    )
    sum_c = Sum(pair_c).halve_mine().halve_give().swap()
    return jnp.concatenate([total_a, sum_b.finish(pair_c[0]), sum_c.finish()], axis=0)


def solution(mesh):
    placed = (P("snap", "space"), P("snap", "space"), P("space"), P())
    return jax.shard_map(
        on_device, mesh=mesh, in_specs=placed, out_specs=P("space", "snap"), check_vma=False
    )
```

```python
import jax
import jax.numpy as jnp
from jax import lax
from jax.experimental import pallas as pl
from jax.experimental.pallas import tpu as pltpu
from jax.sharding import PartitionSpec as P

PEN_LEN = 128
ROWS = 16
COST_SCALE = 1
LIMIT = 50


def xor_send(x, axis, k):
    n = lax.axis_size(axis)
    return lax.ppermute(x, axis, [(i, i ^ k) for i in range(n)])


def params(mebibytes=3):
    return pltpu.CompilerParams(vmem_limit_bytes=mebibytes * 1024 * 1024)


def cost(flops, nbytes):
    return pl.CostEstimate(flops=flops // COST_SCALE, bytes_accessed=nbytes // COST_SCALE, transcendentals=0)


def pack(adjoint, table, where, jobs, tiles):
    halves, _, points = adjoint.shape
    pen_dev = points // PEN_LEN
    share = pen_dev // tiles
    build = table.shape[0] != pen_dev
    magic = (1 << 20) // pen_dev + 1
    exact = all(x * magic >> 20 == x // pen_dev for x in range(tiles * pen_dev))

    def body(table_ref, where_ref, in_ref, *refs):
        outs = refs[: len(jobs)]
        if build:
            made, seen = refs[len(jobs) :]
            place = where_ref[0]
            for k in range(tiles):
                seen[k] = 0

            def enter(q, carry):
                slot = table_ref[place * pen_dev + q]
                k = (slot * magic >> 20 if exact else lax.div(slot, pen_dev)) ^ place
                t = seen[k]
                seen[k] = t + 1
                made[k * share + t] = q
                return carry

            lax.fori_loop(0, pen_dev, enter, 0, unroll=8)
        else:
            made = table_ref
        for o, (k, first, count) in enumerate(jobs):
            for t in range(share):
                start = pl.multiple_of(made[k * share + t] * PEN_LEN, PEN_LEN)
                for h in range(halves):
                    outs[o][h * count : (h + 1) * count, t * PEN_LEN : (t + 1) * PEN_LEN] = in_ref[
                        h, first : first + count, pl.ds(start, PEN_LEN)
                    ]

    smem, vmem = pl.BlockSpec(memory_space=pltpu.SMEM), pl.BlockSpec(memory_space=pltpu.VMEM)
    return pl.pallas_call(
        body,
        in_specs=[smem, smem, vmem],
        out_specs=[vmem] * len(jobs) + [smem] * build,
        out_shape=[jax.ShapeDtypeStruct((halves * count, share * PEN_LEN), jnp.bfloat16) for _, _, count in jobs]
        + [jax.ShapeDtypeStruct((pen_dev,), jnp.int32)] * build,
        scratch_shapes=[pltpu.SMEM((tiles,), jnp.int32)] * build,
        compiler_params=params(),
        cost_estimate=cost(0, 4 * halves * sum(count for _, _, count in jobs) * share * PEN_LEN),
    )(table, where, adjoint)


def slots_of(pencil_map, place, tiles):
    pen_dev = pencil_map.shape[0] // tiles
    share = pen_dev // tiles
    local = pencil_map.reshape(tiles, pen_dev) - place * pen_dev
    here = (local >= 0) & (local < pen_dev)
    q = jnp.arange(pen_dev)
    rank = jnp.sum(here[:, None, :] & (q[None, None, :] < q[None, :, None]), axis=2)
    match = here[:, None, :] & (rank[:, None, :] == jnp.arange(share)[None, :, None])
    table = jnp.sum(jnp.where(match, local[:, None, :], 0), axis=2)
    order = jnp.arange(tiles) ^ place
    picked = jnp.sum(jnp.where(order[:, None, None] == jnp.arange(tiles)[None, :, None], table[None], 0), axis=1)
    return picked.reshape(pen_dev).astype(jnp.int32)


def weigh(primal, weights, table, first, count, tiles):
    rows, points = primal.shape
    share = points // PEN_LEN // tiles
    step = 64 if rows % 64 == 0 else rows

    def body(table_ref, in_ref, w_ref, out):
        for k in range(count):
            for t in range(share):
                start = pl.multiple_of(table_ref[(first + k) * share + t] * PEN_LEN, PEN_LEN)
                scale = w_ref[:, pl.ds(start, PEN_LEN)]
                for i in range(0, rows, step):
                    tile = in_ref[i : i + step, pl.ds(start, PEN_LEN)].astype(jnp.float32) * scale
                    out[k, i : i + step, t * PEN_LEN : (t + 1) * PEN_LEN] = tile.astype(jnp.bfloat16)

    vmem = pl.BlockSpec(memory_space=pltpu.VMEM)
    return pl.pallas_call(
        body,
        in_specs=[pl.BlockSpec(memory_space=pltpu.SMEM), vmem, vmem],
        out_specs=vmem,
        out_shape=jax.ShapeDtypeStruct((count, rows, share * PEN_LEN), jnp.bfloat16),
        compiler_params=params(),
        cost_estimate=cost(rows * points // 2, 3 * rows * points),
    )(table, primal, weights.reshape(1, points))


def merge(parts):
    n = len(parts)
    rows, depth = parts[0].shape
    step = rows // 2 if rows % (2 * ROWS) == 0 else rows

    def body(*refs):
        for i in range(n):
            refs[n][i] = refs[i][...]

    return pl.pallas_call(
        body,
        grid=(rows // step,),
        in_specs=[pl.BlockSpec((step, depth), lambda i: (i, 0))] * n,
        out_specs=pl.BlockSpec((n, step, depth), lambda i: (0, i, 0)),
        out_shape=jax.ShapeDtypeStruct((n, rows, depth), parts[0].dtype),
        compiler_params=params(),
        cost_estimate=cost(0, 4 * n * rows * depth),
    )(*parts)


def whole_rows(stride, first, each):
    return lambda i, h: [(i, h * stride + first, each)]


def multiply(groups, own, other, at_k, where, before, each, halves, members, spread=True):
    held = members // 2
    last = before is not None and spread
    depth = groups[0][0][0].shape[-1]
    columns = own.shape[1]
    flat = [a for g in groups for a in g[0]]
    total_count = sum(g[1] for g in groups)
    rows = halves * each

    def body(where_ref, *refs):
        ins, w_refs = refs[: len(flat)], refs[len(flat) : len(flat) + 2]
        rest, (held_w, sems) = refs[len(flat) + 2 : -2], refs[-2:]
        total = rest[-1]
        copies = [
            [
                pltpu.make_async_copy(w_refs[side].at[at_k + k], held_w.at[k, side], sems.at[k, side])
                for side in range(2)
            ]
            for k in range(total_count)
        ]
        for pair in copies:
            for copy in pair:
                copy.start()
        starts = [h * before[0].shape[1] // halves + before[1] for h in range(halves)] if before is not None else []
        if last:
            for n in range(held):
                for h, start in enumerate(starts):
                    at = n * rows + h * each
                    total[at : at + each, :] = rest[0][n, start : start + each, :]
        k = 0
        for g, (_, count, pieces) in enumerate(groups):
            for i in range(count):
                taken = []
                for ref in ins[g * held : (g + 1) * held]:
                    for h in range(halves):
                        for slot, start, length in pieces(i, h):
                            span = slice(start, start + length)
                            taken.append(ref[slot, span, :] if len(ref.shape) == 3 else ref[span, :])
                stacked = jnp.concatenate(taken, axis=0)
                for side in range(2):
                    copies[k][side].wait()
                    product = lax.dot_general(
                        stacked, held_w[k, side], (((1,), (1,)), ((), ())), preferred_element_type=jnp.float32
                    )
                    span = slice(side * columns, (side + 1) * columns)
                    if last:
                        total[:, span] += product
                    else:
                        for n in range(held):
                            value = product[n * rows : (n + 1) * rows]
                            if k:
                                value = value + total[n, :, span]
                            elif before is not None:
                                value = value + jnp.concatenate([rest[0][n, at : at + each, span] for at in starts], axis=0)
                            total[n, :, span] = value
                k += 1
        if last:
            for n in range(held):
                for h in range(halves):
                    e = ((where_ref[1] ^ (2 * n)) * halves + h) ^ where_ref[0]
                    to, low = lax.div(e, 2 * halves), lax.rem(e, halves)
                    at = (n * halves + h) * each
                    for which in range(halves):

                        @pl.when(low == which)
                        def _(to=to, at=at, which=which):
                            for side in range(2):
                                rest[1 + side * halves + which][to] = total[
                                    at : at + each, side * columns : (side + 1) * columns
                                ]

    vmem, anywhere = pl.BlockSpec(memory_space=pltpu.VMEM), pl.BlockSpec(memory_space=pl.ANY)
    full = jax.ShapeDtypeStruct((held, rows, 2 * columns), jnp.float32)
    split = [jax.ShapeDtypeStruct((held, each, columns), jnp.float32)] * (2 * halves)
    return pl.pallas_call(
        body,
        in_specs=[pl.BlockSpec(memory_space=pltpu.SMEM)]
        + [vmem] * len(flat)
        + [anywhere] * 2
        + [vmem] * (before is not None),
        out_specs=[vmem] * (2 * halves) if last else vmem,
        out_shape=split if last else full,
        scratch_shapes=([pltpu.VMEM((held * rows, 2 * columns), jnp.float32)] if last else [])
        + [pltpu.VMEM((total_count, 2, columns, depth), jnp.bfloat16), pltpu.SemaphoreType.DMA((total_count, 2))],
        compiler_params=params(LIMIT),
        cost_estimate=cost(
            4 * held * rows * columns * depth * total_count, 2 * total_count * depth * (held * rows + 2 * columns)
        ),
    )(where, *flat, own, other, *((before[0],) if before is not None else ()))


def after(x, *done):
    return lax.optimization_barrier((x,) + done)[0] if done else x


def on_device(primal, adjoint_pencils, weights, pencil_map):
    rows_here, points = adjoint_pencils.shape
    tiles = lax.axis_size("space")
    members = lax.axis_size("snap")
    place, lane = lax.axis_index("space"), lax.axis_index("snap")
    where = jnp.stack([place, lane]).astype(jnp.int32)
    rows_out = rows_here * members // tiles
    halves = rows_here // rows_out
    adjoint = adjoint_pencils.reshape(halves, rows_out, points)
    half = tiles // 2
    middle = half + half // 2
    units = rows_out // ROWS
    rows_a = units // 2 * ROWS
    rows_b = max(1, 3 * units // 8) * ROWS
    rows_c = rows_out - rows_a - rows_b
    table = slots_of(pencil_map, place, tiles)

    tables = [pencil_map]

    def pack_rows(source, *runs):
        jobs = [(k, first, count) for first, count, ks in runs for k in ks]
        packed = pack(source, tables[-1], where, jobs, tiles)
        tables.extend(packed[len(jobs) :])
        out = [dict(zip(ks, packed[sum(len(r[2]) for r in runs[:i]) :])) for i, (_, _, ks) in enumerate(runs)]
        return out[0] if len(out) == 1 else out

    def over_space(packed, ks, *done):
        return [xor_send(after(packed[k], *done), "space", k) for k in ks]

    def join(found):
        return found[0] if len(found) == 1 else merge(found)

    def across(block, *done):
        found, bit = [block], members // 2
        order = [0]
        while bit > 1:
            found = found + [xor_send(after(b, *done), "snap", bit) for b in found]
            order = order + [n ^ bit for n in order]
            bit //= 2
        return [found[order.index(n)] for n in sorted(order)]

    def swap_send(x, bit):
        pairs = [(i, i ^ (bit * members + 1)) for i in range(tiles * members)]
        return lax.ppermute(x, ("space", "snap"), pairs)

    same = (((lane * halves) ^ place) & halves) == 0

    class Sum:
        def __init__(self, parts):
            self.mine, self.give = parts[:halves], parts[halves:]

        def halve_mine(self, *done):
            self.got = [xor_send(after(self.mine[low], *done), "space", low) for low in range(1, halves)]
            return self

        def halve_give(self, *done):
            self.got_give = [swap_send(after(self.give[low], *done), low) for low in range(1, halves)]
            return self

        def swap(self, *done):
            self.swapped = xor_send(after(self.give[0], *done), "snap", 1)
            return self

        def finish(self, *done):
            own = sum(self.got, self.mine[0])
            rest = sum(self.got_give, self.swapped)
            zero, one = jnp.where(same, own, rest), jnp.where(same, rest, own)
            total = zero[0]
            self.last = []
            for hi in range(members // 2):
                for core, part in enumerate((zero, one)):
                    if hi or core:
                        self.last.append(xor_send(after(part[hi], *done), "space", halves * (core + 2 * hi)))
            return sum(self.last, total)

    near_a, near_b = list(range(2, 2 + (half - 2) // 2)), list(range(2 + (half - 2) // 2, half))
    low, high = list(range(half, middle)), list(range(middle, tiles))

    rows_bc = rows_b + rows_c
    start_low, rest_low = low[: len(low) // 2], low[len(low) // 2 :]
    early = 2 + len(near_a)

    packed_n, packed_a, packed_na = pack_rows(
        adjoint, (0, rows_out, [0, 1]), (0, rows_a, start_low), (0, rows_a, near_a)
    )
    low_a = over_space(packed_a, start_low)
    got_na = over_space(packed_na, near_a)
    near_1 = over_space(packed_n, [1])[0]
    cross_0 = across(packed_n[0])
    own_1 = weigh(after(primal, packed_na[near_a[0]]), weights, table, 0, early, tiles)
    own_2 = weigh(after(primal, own_1), weights, table, early, tiles - early, tiles)
    packed_ar = pack_rows(after(adjoint, own_2), (0, rows_a, rest_low))
    packed_nr = pack_rows(after(adjoint, packed_ar[rest_low[0]]), (rows_a, rows_bc, near_a))

    done = (*got_na, *low_a, near_1, cross_0[-1], packed_nr[near_a[0]])
    low_a = low_a + over_space(packed_ar, rest_low, *done)
    got_na = got_na + over_space(packed_nr, near_a, *done)
    cross_1 = across(near_1, *done)
    other_1 = xor_send(after(own_1, *done), "snap", 1)
    other_2 = xor_send(after(own_2, *done), "snap", 1)
    packed_nb = pack_rows(after(adjoint, *done), (0, rows_a, near_b))
    packed_ah = pack_rows(after(adjoint, packed_nb[near_b[0]]), (0, rows_a, high))
    packed_bc = pack_rows(after(adjoint, packed_ah[high[0]]), (rows_a, rows_bc, low + near_b))
    packed_b = pack_rows(after(adjoint, packed_bc[low[0]]), (rows_a, rows_b, high))
    packed_c = pack_rows(after(adjoint, packed_b[high[0]]), (rows_a + rows_b, rows_c, high))

    done = (*low_a, *got_na, cross_1[-1], other_1, other_2, packed_c[high[0]])
    high_a = over_space(packed_ah, high, *done)
    got_nb = over_space(packed_nb, near_b, *done)
    cross_low_a = across(join(low_a), *done)
    cross_na = across(join(got_na), *done)

    done = (*high_a, *got_nb, cross_low_a[-1], cross_na[-1])
    low_bc = over_space(packed_bc, low, *done)
    got_nb_bc = over_space(packed_bc, near_b, *done)
    cross_nb = across(join(got_nb), *done)
    cross_high_a = across(join(high_a), *done)

    def two_runs(i, h):
        return [(i, h * rows_a, rows_a), (len(near_a) + i, h * rows_bc, rows_bc)]

    plain = whole_rows(rows_out, 0, rows_out)
    groups = [(cross_0, 1, plain), (cross_1, 1, plain), (cross_na, len(near_a), two_runs)]
    product = multiply(groups, own_1, after(other_1, *done), 0, where, None, rows_out, halves, members)

    done = (*got_nb_bc, *low_bc, cross_nb[-1], cross_high_a[-1], product)
    high_b = over_space(packed_b, high, *done)
    cross_low_bc = across(join(low_bc), *done)
    cross_nb_bc = across(join(got_nb_bc), *done)
    rows = whole_rows(rows_a, 0, rows_a)
    groups = [(cross_nb, len(near_b), rows), (cross_low_a, len(low), rows), (cross_high_a, len(high), rows)]
    pair_a = multiply(groups, own_2, other_2, 0, where, (product, 0), rows_a, halves, members)

    sum_a = Sum(pair_a).halve_mine()

    done = (*high_b, cross_low_bc[-1], cross_nb_bc[-1], pair_a[0], *sum_a.got)
    high_c = over_space(packed_c, high, *done)
    cross_high_b = across(join(high_b), *done)
    sum_a.halve_give(*done).swap(*done)
    rows = whole_rows(rows_bc, 0, rows_bc)
    groups = [(cross_nb_bc, len(near_b), rows), (cross_low_bc, len(low), rows)]
    first_high = len(near_b) + len(low)
    product_bc = multiply(
        groups, own_2, after(other_2, *done), 0, where, (product, rows_a), rows_bc, halves, members, False
    )

    done = (*high_c, cross_high_b[-1], *sum_a.got_give, sum_a.swapped, product_bc)
    cross_high_c = across(join(high_c), *done)
    total_a = sum_a.finish(*done)
    groups = [(cross_high_b, len(high), whole_rows(rows_b, 0, rows_b))]
    pair_b = multiply(groups, own_2, after(other_2, *done), first_high, where, (product_bc, 0), rows_b, halves, members)
    crossed = cross_high_c[-1]
    sum_b = Sum(pair_b).halve_mine(cross_high_c[-1]).halve_give(cross_high_c[-1]).swap(cross_high_c[-1])
    groups = [(cross_high_c, len(high), whole_rows(rows_c, 0, rows_c))]
    pair_c = multiply(
        groups, own_2, after(other_2, *sum_a.last[::2], sum_b.swapped), first_high, where, (product_bc, rows_b), rows_c, halves, members
    )
    sum_c = Sum(pair_c).halve_mine().halve_give().swap()
    return jnp.concatenate([total_a, sum_b.finish(pair_c[0]), sum_c.finish()], axis=0)


def solution(mesh):
    placed = (P("snap", "space"), P("snap", "space"), P("space"), P())
    return jax.shard_map(
        on_device, mesh=mesh, in_specs=placed, out_specs=P("space", "snap"), check_vma=False
    )
```
